32 devices in a mesh: loop: 4 (over y, x), group: 8 (over z, core).
Axes of the slice: x: 2, y: 2, z: 4, core: 2. Of those that a mesh axis runs over, the one named last changes fastest.
Arguments:
- view_embeds: bfloat16 [32768, 1152], P(('loop', 'group')), may hold values from -0.1875 to 0.1875
- view_image: int32 [32768], P(('loop', 'group')), may hold values from 0 to 8191, as said below
- view_counts: int32 [8192], P(('loop', 'group')), may hold values from 2 to 6, as said below
- text_feats: bfloat16 [8192, 1152], P(('loop', 'group')), may hold values from -0.1875 to 0.1875
- head_weight: bfloat16 [1152, 1152], replicated, may hold values from -0.1875 to 0.1875
- logit_scale: float32 [1], replicated, may hold values from 5 to 15
- logit_bias: float32 [1], replicated, may hold values from -3 to -1
Outputs:
- view_grad: bfloat16 [32768, 1152], P(('loop', 'group'))
- view_loss: bfloat16 [32768], P(('loop', 'group'))
- text_grad: bfloat16 [8192, 1152], P(('loop', 'group'))
- head_grad: float32 [1152, 1152], P('group')
The draws below stay inside these ranges and needn't reach their ends.
Inputs may be any that keep to these rules, and one draw needn't show every extreme that they name: view_counts[i] is the number of rows of view_image that name image i. `view_image`: the 1024 rows of one device name only images whose captions lie on a device with the same loop index. At most 176 of one device's rows name images held by any one device, and in every draw some devices hold images named by exactly 176 rows of every device with their loop index. The images of one loss group have 4096 view rows in all.
All inputs are finite; a program needn't handle non-finite values.
Results may differ from the reference program's by a relative error of at most 0.015.
Values may be sent and summed in bfloat16 or wider, within the bound.
No kernel may reach another device: no remote copies, remote signals or barrier semaphores. Data moves between devices by JAX's collectives and lax.ppermute only.
A program may use at most 128 MiB of HBM per device.

```python
import jax
import jax.numpy as jnp
from jax import lax

D = 1152
CAP = 256
GROUP_CAPS = 1024
GROUP_VIEWS = 4096
IMAGES = 8192
VIEWS = 32768
N_LOOP = 4
N_GROUP = 8


def view_layout(key):
    subkeys = jax.random.split(jax.random.fold_in(key, 11), 4)
    holders = N_LOOP * N_GROUP
    loop_sign = jnp.where(jax.random.permutation(subkeys[0], N_LOOP) < N_LOOP // 2, 1, -1).astype(jnp.int32)
    group_sign = jnp.where(jax.random.permutation(subkeys[1], N_GROUP) < N_GROUP // 2, 1, -1).astype(jnp.int32)
    holder_sign = (loop_sign[:, None] * group_sign[None, :]).reshape(holders)
    shuffled = jax.vmap(lambda sub_key: jax.random.permutation(sub_key, CAP))(jax.random.split(subkeys[2], holders))
    further = (shuffled < CAP // 2).astype(jnp.int32)
    counts = (4 + holder_sign[:, None] * (1 + further)).astype(jnp.int32)
    slot_count = 11 * CAP // (2 * N_GROUP)
    running = jnp.cumsum(counts, axis=1).reshape(N_LOOP, N_GROUP, CAP)
    per_source = running[:, :, CAP - 1] // N_GROUP
    source_index = jnp.arange(N_GROUP, dtype=jnp.int32)
    within = jnp.arange(slot_count, dtype=jnp.int32)
    wanted = source_index[None, None, :, None] * per_source[:, :, None, None] + within[None, None, None, :]
    alive_slot = jnp.broadcast_to(within[None, None, None, :] < per_source[:, :, None, None], wanted.shape)

    def locate(bounds, targets):
        return jnp.searchsorted(bounds, targets, side='right').astype(jnp.int32)
    local_image = jnp.minimum(jax.vmap(jax.vmap(locate))(running, wanted), CAP - 1)
    holder_index = jnp.arange(N_LOOP, dtype=jnp.int32)[:, None] * N_GROUP + jnp.arange(N_GROUP, dtype=jnp.int32)[None, :]
    image_ids = holder_index[:, :, None, None] * CAP + local_image
    image_ids = jnp.transpose(image_ids, (0, 2, 1, 3)).reshape(holders, N_GROUP * slot_count)
    alive_slot = jnp.transpose(alive_slot, (0, 2, 1, 3)).reshape(holders, N_GROUP * slot_count)
    rows_device = 4 * CAP

    def compact(values, alive, sub_key):
        ordering = jnp.argsort(jnp.where(alive, 0, 1).astype(jnp.int32), stable=True)[:rows_device]
        mixing = jax.random.permutation(sub_key, rows_device)
        return values[ordering][mixing]
    row_images = jax.vmap(compact)(image_ids, alive_slot, jax.random.split(subkeys[3], holders))
    return (counts.reshape(holders * CAP).astype(jnp.int32), row_images.reshape(holders * rows_device).astype(jnp.int32))


def draw_view_counts(key, part):
    return view_layout(key)[0]


def draw_view_image(key, part):
    return view_layout(key)[1]


def level_of(own_key, dims, cuts, low, high):
    level, own = 1.0, jax.random.fold_in(own_key, 6)
    for axis_at, parts in cuts:
        heights = jnp.exp(jax.random.uniform(jax.random.fold_in(own, axis_at), (parts,), jnp.float32, low / len(cuts), high / len(cuts)))
        level = level * jnp.repeat(heights, dims[axis_at] // parts).reshape([-1 if axis == axis_at else 1 for axis in range(len(dims))])
    return level


def bell_draw(stream_key, extent, spread, reach, cuts=(), kind=jnp.bfloat16):
    array = jax.random.normal(stream_key, extent, jnp.float32) * spread
    if len(cuts) > 0:
        array = level_of(stream_key, extent, cuts, -0.22, 0.18) * array
    return jnp.clip(array, min=-reach, max=reach).astype(kind)


def setup_inputs(seed: int = 0) -> dict:
    keys = jax.random.split(jax.random.key(seed), 8)
    return {
        "view_embeds": bell_draw(keys[0], (VIEWS, D), D ** -0.5, 0.1875, ((0, 32),)),
        "view_image": draw_view_image(jax.random.fold_in(keys[7], 71), 0),
        "view_counts": draw_view_counts(jax.random.fold_in(keys[7], 71), 0),
        "text_feats": bell_draw(keys[3], (IMAGES, D), D ** -0.5, 0.1875, ((0, 32),)),
        "head_weight": bell_draw(keys[4], (D, D), D ** -0.5, 0.1875),
        "logit_scale": jnp.clip(jax.random.uniform(keys[5], (1,), jnp.float32, 5.0, 15.0), 5.0, 15.0),
        "logit_bias": jnp.clip(jax.random.uniform(keys[6], (1,), jnp.float32, -3.0, -1.0), -3.0, -1.0),
    }


epsilon = 1e-06

def unit_rows(values):
    inverse = lax.rsqrt(lax.optimization_barrier(jnp.sum(values * values, axis=1, keepdims=True)) + epsilon)
    return (values * inverse, inverse)

def reference(view_embeds, view_image, view_counts, text_feats, head_weight, logit_scale, logit_bias):
    logit_mult = logit_scale[0]
    offset = logit_bias[0]
    x_unit, inv_x = unit_rows(view_embeds.astype(jnp.float32))
    x_half = x_unit.astype(jnp.bfloat16)
    text_embed = jnp.dot(text_feats, head_weight, preferred_element_type=jnp.float32)
    y_unit, inv_y = unit_rows(text_embed)
    y_half = y_unit.astype(jnp.bfloat16)
    row_weight = 1.0 / view_counts[view_image].astype(jnp.float32)
    block_index = view_image // CAP
    loss_group = (block_index % N_GROUP).astype(jnp.int32)
    column = (block_index // N_GROUP * CAP + view_image % CAP).astype(jnp.int32)
    ordering = jnp.argsort(loss_group, stable=True).astype(jnp.int32)
    group_rows = ordering.reshape(N_GROUP, GROUP_VIEWS)
    group_captions = jnp.transpose(y_half.reshape(N_LOOP, N_GROUP, CAP, D), (1, 0, 2, 3)).reshape(N_GROUP, GROUP_CAPS, D)
    caption_ids = jnp.arange(GROUP_CAPS, dtype=jnp.int32)

    def one_group(inputs):
        row_ids, captions = inputs
        x_rows = x_half[row_ids]
        scores = jnp.dot(x_rows, captions.T, preferred_element_type=jnp.float32)
        labels = jnp.where(column[row_ids][:, None] == caption_ids[None, :], 1.0, -1.0)
        margin = -labels * (logit_mult * scores + offset)
        loss_rows = lax.optimization_barrier(jnp.sum(jax.nn.softplus(margin), axis=1)) / GROUP_CAPS
        pair_grad = (row_weight[row_ids][:, None] * logit_mult * -labels * jax.nn.sigmoid(margin)).astype(jnp.bfloat16)
        view_part = jnp.dot(pair_grad, captions, preferred_element_type=jnp.float32)
        caption_part = jnp.dot(pair_grad.T, x_rows, preferred_element_type=jnp.float32)
        return (loss_rows, view_part, caption_part)
    loss_rows, view_part, caption_part = lax.map(one_group, (group_rows, group_captions))
    gx_unit = jnp.zeros((VIEWS, D), jnp.float32).at[ordering].set(view_part.reshape(VIEWS, D))
    loss_all = jnp.zeros((VIEWS,), jnp.float32).at[ordering].set(loss_rows.reshape(VIEWS))
    view_grad = ((gx_unit - x_unit * lax.optimization_barrier(jnp.sum(x_unit * gx_unit, axis=1, keepdims=True))) * inv_x).astype(jnp.bfloat16)
    view_loss = loss_all.astype(jnp.bfloat16)
    gy_unit = jnp.transpose(caption_part.reshape(N_GROUP, N_LOOP, CAP, D), (1, 0, 2, 3)).reshape(IMAGES, D)
    caption_grad = (gy_unit - y_unit * lax.optimization_barrier(jnp.sum(y_unit * gy_unit, axis=1, keepdims=True))) * inv_y
    grad_half = caption_grad.astype(jnp.bfloat16)
    text_grad = jnp.dot(grad_half, head_weight.T, preferred_element_type=jnp.float32).astype(jnp.bfloat16)
    head_grad = jnp.dot(text_feats.T, grad_half, preferred_element_type=jnp.float32)
    return (view_grad, view_loss, text_grad, head_grad)
```

```python
import functools

import jax
import jax.numpy as jnp
from jax import lax
from jax.experimental import pallas as pl
from jax.experimental.pallas import tpu as pltpu
from jax.sharding import PartitionSpec as P

epsilon = 1e-06
mates = 4
f32 = jnp.float32
bf16 = jnp.bfloat16
NN = (((1,), (0,)), ((), ()))
NT = (((1,), (1,)), ((), ()))


def dot(a, b, dims):
    return lax.dot_general(a, b, dims, preferred_element_type=f32)


def params(mib, **more):
    return pltpu.CompilerParams(vmem_limit_bytes=mib << 20, **more)


VMEM = pl.BlockSpec(memory_space=pltpu.VMEM)
SMEM = pl.BlockSpec(memory_space=pltpu.SMEM)


def log2_of(value):
    bits = value.bit_length() - 1
    assert 1 << bits == value
    return bits


def slot_ids(targets, rank, cluster, place, slots):
    mate = (targets & (mates - 1)) ^ place
    q = (targets >> 2) ^ cluster
    return (q * mates + mate) * slots + rank


def pack_kernel(cap, groups, slots, parts, members, where_ref, image_ref, views_ref, *refs):
    rows, width = views_ref.shape
    image = image_ref[...]
    if len(refs) > len(members):
        sid_ref, out_refs = refs[0], refs[1:]
        targets = (image >> log2_of(cap)) & (groups - 1)
        wide = max(groups, 16)
        chosen = (lax.broadcasted_iota(jnp.int32, (wide, rows), 0) == targets).astype(f32)
        before = (
            lax.broadcasted_iota(jnp.int32, (rows, rows), 0)
            < lax.broadcasted_iota(jnp.int32, (rows, rows), 1)
        ).astype(f32).astype(bf16)
        earlier = dot(chosen.astype(bf16), before, NN)
        rank = jnp.sum(earlier * chosen, axis=0, keepdims=True).astype(jnp.int32)
        sid = slot_ids(targets, rank, where_ref[0], where_ref[1], slots)
        sid_ref[...] = sid
    else:
        sid, out_refs = where_ref[...], refs
    local = (image & (cap - 1)).astype(f32)
    line = lax.broadcasted_iota(jnp.int32, (16, rows), 0)
    views = views_ref[...]
    slot = lax.broadcasted_iota(jnp.int32, (slots, rows), 0)
    for n, m in enumerate(members):
        hots = [(slot == sid - (q * mates + m) * slots).astype(f32).astype(bf16) for q in range(parts)]
        packed = dot(jnp.concatenate(hots, axis=0), views, NN)
        lines = jnp.zeros((16, slots), f32)
        for q, hot in enumerate(hots):
            info = jnp.where(line == q, local, jnp.where(line == parts + q, 1.0, 0.0)).astype(bf16)
            lines += dot(info, hot, NT)
        out_refs[n][: parts * slots, :] = packed.astype(bf16)
        out_refs[n][parts * slots :, :] = jnp.zeros((16, width), bf16)
        out_refs[n][parts * slots :, :slots] = lines.astype(bf16)


def caption_kernel(counts, weight_ref, *refs):
    feats, (half_ref, unit_ref, inverse_ref, turned_ref) = refs[:-4], refs[-4:]

    def block(pieces):
        value = jnp.concatenate([ref[...] for ref in pieces], axis=0)
        embed = dot(value, weight_ref[...], NN)
        inverse = lax.rsqrt(jnp.sum(embed * embed, axis=1, keepdims=True) + epsilon)
        unit = embed * inverse
        half_ref[...] = unit.astype(bf16)
        unit_ref[...] = unit
        inverse_ref[...] = jnp.broadcast_to(inverse, inverse_ref.shape)
        turned_ref[...] = value.T

    start = 0
    for k, count in enumerate(counts):
        pl.when(pl.program_id(0) == k)(functools.partial(block, feats[start : start + count]))
        start += count


def score_kernel(cap, q, parts, priors, scale_ref, offset_ref, a_ref, b_ref, ia_ref, ib_ref, count_ref, caps_ref, *refs):
    prior_refs, (va_ref, vb_ref, turned_ref, half_ref, loss_ref, pair_ref) = refs[:-6], refs[-6:]
    pair, slots = loss_ref.shape[:2]
    caps, width = caps_ref.shape
    scale, offset = scale_ref[0], offset_ref[0]
    eye = lax.broadcasted_iota(jnp.int32, (slots, slots), 0) == lax.broadcasted_iota(
        jnp.int32, (slots, slots), 1
    )
    held = [
        dot(eye.astype(f32).astype(bf16), ref[:, :slots], NT) for ref in (ia_ref, ib_ref)
    ]
    held = jnp.concatenate(held, axis=0)
    column = jnp.where(held[:, parts + q : parts + q + 1] > 0.5, held[:, q : q + 1], -1.0)
    named = lax.broadcasted_iota(jnp.int32, (pair * slots, cap), 1).astype(f32) == column
    weight = jnp.sum(
        jnp.where(named, 1.0 / count_ref[...].astype(f32), 0.0), axis=1, keepdims=True
    )
    factor = weight * scale
    x = jnp.concatenate([a_ref[...], b_ref[...]], axis=0).astype(f32)
    inverse = lax.rsqrt(jnp.sum(x * x, axis=1, keepdims=True) + epsilon)
    unit = x * inverse
    half = unit.astype(bf16)
    half_ref[: pair * slots, :] = half
    half_ref[pair * slots :, :] = jnp.zeros((half_ref.shape[0] - pair * slots, width), bf16)
    loss = jnp.zeros((pair * slots, 1), f32)
    for k in range(caps // cap):
        here = pl.ds(k * cap, cap)
        value = dot(half, caps_ref[here, :], NT) * scale + offset
        if k == 0:
            margin = jnp.where(named, -value, value)
        else:
            margin = value
        e = jnp.exp(-jnp.abs(margin))
        u = 1.0 + e
        r = 1.0 / u
        log1p = jnp.log(u) + (e - (u - 1.0)) * r
        loss = loss + jnp.sum(jnp.maximum(margin, 0.0) + log1p, axis=1, keepdims=True)
        grad = factor * jnp.where(margin >= 0.0, r, e * r)
        if k == 0:
            grad = jnp.where(named, -grad, grad)
        pair_ref[:, here] = grad.astype(bf16)
        turned_ref[here, : pair * slots] = grad.T.astype(bf16)
        turned_ref[here, pair * slots :] = jnp.zeros((cap, turned_ref.shape[1] - pair * slots), bf16)
    grad_x = dot(pair_ref[...], caps_ref[...], NN)
    grad_v = (grad_x - unit * jnp.sum(unit * grad_x, axis=1, keepdims=True)) * inverse
    grad_v = grad_v.astype(bf16)
    loss = loss * (1.0 / caps)
    for m, back_ref in enumerate((va_ref, vb_ref)):
        back_ref[:slots, :] = grad_v[m * slots : (m + 1) * slots]
    for m in range(pair):
        loss_ref[m] = jnp.broadcast_to(loss[m * slots : (m + 1) * slots], (slots, 128))
    if va_ref.shape[0] > slots:
        ones = jnp.ones((16, slots), bf16)
        line = lax.broadcasted_iota(jnp.int32, (16, slots), 0)
        for m, back_ref in enumerate((va_ref, vb_ref)):
            columns = [(p, ref[m][:, 0:1]) for p, ref in zip(priors, prior_refs)]
            columns.append((q, loss[m * slots : (m + 1) * slots]))
            lines = jnp.zeros((16, slots), f32)
            for p, value in columns:
                lines += jnp.where(line == p, dot(ones, jnp.where(eye, value, 0.0).astype(bf16), NN), 0.0)
            back_ref[slots:, :] = jnp.zeros((16, width), bf16)
            back_ref[slots:, :slots] = lines.astype(bf16)


def caption_grad_kernel(pa_ref, pb_ref, xa_ref, xb_ref, unit_ref, inverse_ref, out_ref):
    pairs = jnp.concatenate([pa_ref[...], pb_ref[...]], axis=1)
    total = dot(pairs, jnp.concatenate([xa_ref[...], xb_ref[...]], axis=0), NN)
    unit = unit_ref[...]
    total = total - unit * jnp.sum(unit * total, axis=1, keepdims=True)
    out_ref[...] = (total * inverse_ref[:, 0:1]).astype(bf16)


def unpack_kernel(slots, parts, part, sid_ref, *refs):
    backs, refs = refs[:mates], refs[mates:]
    rows = sid_ref.shape[1]
    last = len(refs) > 1
    many = mates * slots
    sid = jnp.broadcast_to(sid_ref[...].astype(f32), (128, rows)).T[:, 0:1].astype(jnp.int32)
    lanes = lax.broadcasted_iota(jnp.int32, (rows, many), 1)

    def hot(q):
        return (lanes == sid - q * many).astype(f32).astype(bf16)

    back = jnp.concatenate([ref[:slots, :] for ref in backs], axis=0)
    result = dot(hot(part), back, NN)
    if last:
        lines, (before_ref, out_ref, loss_ref) = refs[:mates], refs[mates:]
        result = result + before_ref[...].astype(f32)
    else:
        (out_ref,) = refs
    out_ref[...] = result.astype(bf16)
    if last:
        losses = jnp.zeros((16, rows), f32)
        for q in range(parts):
            line = jnp.concatenate([ref[:, :slots] for ref in lines], axis=1)
            mine = lax.broadcasted_iota(jnp.int32, line.shape, 0) == q
            line = jnp.where(mine, line.astype(f32), 0.0).astype(bf16)
            losses += dot(line, hot(q), NT)
        loss_ref[...] = jnp.sum(losses, axis=0, keepdims=True)


def after(value, *others):
    return lax.optimization_barrier((value, *others))[0]


def with_order(kernel, count):
    return lambda *refs: kernel(*refs[count:])


ANY = pl.BlockSpec(memory_space=pl.ANY)


def cost(flops, read, wrote):
    return pl.CostEstimate(flops=flops, bytes_accessed=read + wrote, transcendentals=0)


def local(view_embeds, view_image, view_counts, text_feats, head_weight, logit_scale, logit_bias):
    cap = view_counts.shape[0]
    rows, width = view_embeds.shape
    groups = lax.axis_size("group")
    loops = lax.axis_size("loop")
    parts = groups // mates
    slots = -(-(11 * cap // (2 * groups)) // 16) * 16
    pair_slots = -(-2 * slots // 128) * 128
    caps = cap * loops
    me = lax.axis_index("group")
    lane = lax.axis_index("loop")
    cluster, place = me // mates, me % mates

    def over(axis, size, value, mask):
        return lax.ppermute(value, axis, [(i, i ^ mask) for i in range(size)])

    def over_loop(value, mask):
        return over("loop", loops, value, mask)

    def over_group(value, mask):
        return over("group", groups, value, mask)

    def bits_of(k):
        return [1 << b for b in range(k.bit_length()) if k >> b & 1][:2]

    in_order = sorted(range(1, loops), key=lambda k: (bin(k).count("1"), k))

    def gather_loop(block):
        pieces = {0: [block]}
        for k in in_order:
            bits = bits_of(k)
            if len(bits) == 1:
                pieces[k] = [over_loop(block, k)]
                continue
            pieces[k] = []
            for i, bit in enumerate(bits):
                source = pieces[k ^ bit]
                half = source[i] if len(source) == 2 else lax.slice_in_dim(source[0], i * cap // 2, (i + 1) * cap // 2)
                pieces[k].append(over_loop(half, bit))
        return pieces

    def scatter_loop(terms):
        half = cap // 2
        total = {(k, i): terms[k, i * half : (i + 1) * half] for k in range(loops) for i in range(2)}
        bit = {(k, i): bits_of(k)[i % len(bits_of(k))] for k, i in total if k}
        children = {at: [way for way in bit if way[1] == at[1] and way[0] ^ bit[way] == at[0]] for at in total}

        def depth(at):
            return 1 + max((depth(child) for child in children[at]), default=-1)

        waves = {}
        for at in bit:
            waves.setdefault((depth(at), bit[at]), []).append(at)
        marks = []
        for (_, way), members in sorted(waves.items()):
            sent = [total[at].astype(bf16) for at in members]
            got = over_loop(jnp.concatenate(sent) if len(sent) > 1 else sent[0], way)
            marks.append(got)
            for n, (k, i) in enumerate(members):
                parent = (k ^ way, i)
                total[parent] = total[parent].astype(f32) + got[n * half : (n + 1) * half].astype(f32)
        return jnp.concatenate([total[0, 0], total[0, 1]], axis=0), marks

    where = jnp.stack([cluster, place]).astype(jnp.int32)

    feats = [text_feats] + [over_group(text_feats, mates * q) for q in range(1, parts)]
    counts = [view_counts] + [over_group(view_counts, mates * q) for q in range(1, parts)]
    counts = [value.reshape(1, cap) for value in counts]

    row = jax.ShapeDtypeStruct((parts * slots + 16, width), bf16)
    def pack(members, where, *more):
        many = parts * len(members) * slots
        return pl.pallas_call(
            functools.partial(pack_kernel, cap, groups, slots, parts, members),
            out_shape=list(more) + [row] * len(members),
            in_specs=[SMEM if more else VMEM, VMEM, VMEM],
            out_specs=[VMEM] * (len(more) + len(members)),
            compiler_params=params(56),
            cost_estimate=cost(2 * many * rows * width, rows * width * 2, many * width * 2),
            name="pack",
        )(where, view_image.reshape(1, rows), view_embeds)

    sid, *far_rows = pack((2, 3), where, jax.ShapeDtypeStruct((1, rows), jnp.int32))
    packed = [*pack((0, 1), sid), *far_rows]
    moved = {m: over_group(packed[m], m) for m in (2, 3, 1)}
    held = [packed[0]] + [moved[m] for m in range(1, mates)]

    def caption(q, gathered, *before):
        pieces = [piece for k in range(loops) for piece in gathered[k]]
        return (
            pl.pallas_call(
                with_order(
                    functools.partial(caption_kernel, [len(gathered[k]) for k in range(loops)]), len(before)
                ),
                grid=(loops,),
                out_shape=[
                    jax.ShapeDtypeStruct((caps, width), bf16),
                    jax.ShapeDtypeStruct((caps, width), f32),
                    jax.ShapeDtypeStruct((caps, 128), f32),
                    jax.ShapeDtypeStruct((width, caps), bf16),
                ],
                in_specs=[ANY] * len(before)
                + [pl.BlockSpec(value.shape, lambda k: (0, 0)) for value in [head_weight, *pieces]],
                out_specs=[pl.BlockSpec((cap, wide), lambda k: (k, 0)) for wide in (width, width, 128)]
                + [pl.BlockSpec((width, cap), lambda k: (0, k))],
                compiler_params=params(56),
                cost_estimate=cost(2 * caps * width * width, (caps + width) * width * 2, caps * width * 8),
                name="captions",
            )(*before, head_weight, *pieces)
        )

    def score(q, first, losses, *before):
        carry = len(losses) == parts - 1
        priors = list(losses) if carry else []
        sent = jax.ShapeDtypeStruct((slots + (16 if carry else 0), width), bf16)
        return pl.pallas_call(
            with_order(functools.partial(score_kernel, cap, q, parts, priors), len(before)),
            grid=(1,),
            out_shape=[
                sent,
                sent,
                jax.ShapeDtypeStruct((caps, pair_slots), bf16),
                jax.ShapeDtypeStruct((pair_slots, width), bf16),
                jax.ShapeDtypeStruct((2, slots, 128), f32),
            ],
            in_specs=[ANY] * len(before)
            + [
                SMEM,
                SMEM,
                pl.BlockSpec((slots, width), lambda i: (q, 0)),
                pl.BlockSpec((slots, width), lambda i: (q, 0)),
                pl.BlockSpec((16, width), lambda i: (parts * slots // 16, 0)),
                pl.BlockSpec((16, width), lambda i: (parts * slots // 16, 0)),
                pl.BlockSpec((1, cap), lambda i: (0, 0)),
                pl.BlockSpec((caps, width), lambda i: (0, 0)),
            ]
            + [pl.BlockSpec((2, slots, 128), lambda i: (0, 0, 0))] * len(priors),
            scratch_shapes=[pltpu.VMEM((2 * slots, caps), bf16)],
            compiler_params=params(56),
            cost_estimate=cost(8 * slots * caps * width, (2 * slots + caps) * width * 2, slots * width * 12),
            name="score",
        )(
            *before, logit_scale, logit_bias, *[held[first + i % 2] for i in range(4)], counts[q], captions[q][0],
            *[losses[p] for p in priors],
        )

    def caption_grad(q, near, far, *before):
        return pl.pallas_call(
            with_order(caption_grad_kernel, len(before)),
            grid=(loops,),
            out_shape=jax.ShapeDtypeStruct((caps, width), bf16),
            in_specs=[ANY] * len(before)
            + [
                pl.BlockSpec((cap, pair_slots), lambda k: (k, 0)),
                pl.BlockSpec((cap, pair_slots), lambda k: (k, 0)),
                pl.BlockSpec((pair_slots, width), lambda k: (0, 0)),
                pl.BlockSpec((pair_slots, width), lambda k: (0, 0)),
                pl.BlockSpec((cap, width), lambda k: (k, 0)),
                pl.BlockSpec((cap, 128), lambda k: (k, 0)),
            ],
            out_specs=pl.BlockSpec((cap, width), lambda k: (k, 0)),
            compiler_params=params(56),
            cost_estimate=cost(
                2 * mates * slots * caps * width, caps * width * 4 + mates * slots * width * 4, caps * width * 2
            ),
            name="caption_grad",
        )(*before, near[2], far[2], near[3], far[3], captions[q][1], captions[q][2])

    def unpack(q, result, *before):
        last = result is not None
        whole = pl.BlockSpec((rows, width), lambda i: (0, 0))
        line = pl.BlockSpec((1, rows), lambda i: (0, 0))
        return pl.pallas_call(
            with_order(functools.partial(unpack_kernel, slots, parts, q), len(before)),
            grid=(1,),
            out_shape=[jax.ShapeDtypeStruct((rows, width), bf16)]
            + [jax.ShapeDtypeStruct((1, rows), f32)] * last,
            in_specs=[ANY] * len(before)
            + [line]
            + [pl.BlockSpec((slots, width), lambda i: (0, 0))] * mates
            + [pl.BlockSpec((16, width), lambda i: (slots // 16, 0))] * (mates * last)
            + [whole] * last,
            out_specs=[whole] + [line] * last,
            compiler_params=params(56),
            cost_estimate=cost(2 * mates * slots * rows * width, mates * slots * width * 2, rows * width * 2),
            name="unpack",
        )(*before, sid, *back[q], *(carriers + [result] if last else []))

    captions, near, far, grads, back, sums, marks = {}, {}, {}, {}, {}, {}, {}
    there = {q: {} for q in range(parts)}
    token = packed[:1]
    for q in range(parts):
        gathered = gather_loop(after(feats[q], token[0]) if q else feats[q])
        captions[q] = caption(q, gathered, *token)
        token = [captions[q][2]]
        if q < parts - 1:
            near[q] = score(q, 0, {p: near[p][4] for p in near}, *token)
            there[q][1] = over_group(near[q][1], 1)
            token = [near[q][4], there[q][1]]
            if q:
                token = token[:1]
    for q in reversed(range(parts)):
        far[q] = score(q, 2, {p: far[p][4] for p in far}, *token)
        there[q][2], there[q][3] = over_group(far[q][0], 2), over_group(far[q][1], 3)
        token = []
        if q == parts - 1:
            near[q] = score(q, 0, {p: near[p][4] for p in near}, far[q][4])
            there[q][1] = over_group(near[q][1], 1)
            token = [there[q][1]]
        back[q] = [near[q][0], there[q][1], there[q][2], there[q][3]]
        grads[q] = caption_grad(q, near[q], far[q])
        token.append(grads[q])
        sums[q], marks[q] = scatter_loop(grads[q].reshape(loops, cap, width))
    carriers = back[parts - 1][:2] + back[0][2:]

    total = sums[0]
    for q in range(1, parts):
        total = total + over_group(sums[q].astype(bf16), mates * q).astype(f32)
    text_grad = jnp.einsum(
        "cd,ed->ce", total.astype(bf16), head_weight, preferred_element_type=f32
    ).astype(bf16)

    share = width // groups
    head = sum(
        dot(captions[q][3], after(grads[q], *marks[parts - 1][:2]), NN) for q in range(parts)
    )
    head = head.astype(bf16)
    head = after(head, *marks[parts - 1][2:], *back[parts - 1][2:])
    head = head.reshape(groups // 2, 2, share, width)
    core = me % 2
    got = over_group(lax.dynamic_index_in_dim(head, 1 - core, 1, keepdims=False), 1)
    head = lax.dynamic_index_in_dim(head, core, 1, keepdims=False).astype(f32) + got.astype(f32)
    head = head.astype(bf16).reshape(groups // 2, loops, share // loops, width)
    piece = lax.dynamic_index_in_dim(head, lane, 1, keepdims=False).astype(f32)
    for k in range(1, loops):
        piece += over_loop(lax.dynamic_index_in_dim(head, lane ^ k, 1, keepdims=False), k).astype(f32)
    head = piece.astype(bf16)
    height = me // 2
    piece = lax.dynamic_index_in_dim(head, height, 0, keepdims=False).astype(f32)
    for k in range(1, groups // 2):
        piece += over_group(lax.dynamic_index_in_dim(head, height ^ k, 0, keepdims=False), 2 * k).astype(f32)
    piece = piece.astype(bf16)
    whole = jnp.stack([piece] + [over_loop(piece, k) for k in range(1, loops)])
    whole = whole[lane ^ jnp.arange(loops, dtype=jnp.int32)]
    head_grad = whole.reshape(share, width).astype(f32)

    result = None
    for q in reversed(range(parts)):
        result = unpack(q, result[0] if result else None)
    view_grad, view_loss = result
    view_loss = view_loss.reshape(rows).astype(bf16)
    return (view_grad, view_loss, text_grad, head_grad)


def solution(mesh):
    return jax.shard_map(
        local,
        mesh=mesh,
        in_specs=(
            P(("loop", "group"), None),
            P(("loop", "group")),
            P(("loop", "group")),
            P(("loop", "group"), None),
            P(),
            P(),
            P(),
        ),
        out_specs=(
            P(("loop", "group"), None),
            P(("loop", "group")),
            P(("loop", "group"), None),
            P("group", None),
        ),
        check_vma=False,
    )
```

```python
import functools

import jax
import jax.numpy as jnp
from jax import lax
from jax.experimental import pallas as pl
from jax.experimental.pallas import tpu as pltpu
from jax.sharding import PartitionSpec as P

epsilon = 1e-06
mates = 4
f32 = jnp.float32
bf16 = jnp.bfloat16
NN = (((1,), (0,)), ((), ()))
NT = (((1,), (1,)), ((), ()))


def dot(a, b, dims):
    return lax.dot_general(a, b, dims, preferred_element_type=f32)


def params(mib, **more):
    return pltpu.CompilerParams(vmem_limit_bytes=mib << 20, **more)


VMEM = pl.BlockSpec(memory_space=pltpu.VMEM)
SMEM = pl.BlockSpec(memory_space=pltpu.SMEM)


def log2_of(value):
    bits = value.bit_length() - 1
    assert 1 << bits == value
    return bits


def slot_ids(targets, rank, cluster, place, slots):
    mate = (targets & (mates - 1)) ^ place
    q = (targets >> 2) ^ cluster
    return (q * mates + mate) * slots + rank


def pack_kernel(cap, groups, slots, parts, where_ref, image_ref, views_ref, sid_ref, own_ref, core_ref, far_ref):
    rows, width = views_ref.shape
    image = image_ref[...]
    targets = (image >> log2_of(cap)) & (groups - 1)
    wide = max(groups, 16)
    chosen = (lax.broadcasted_iota(jnp.int32, (wide, rows), 0) == targets).astype(f32)
    before = (
        lax.broadcasted_iota(jnp.int32, (rows, rows), 0)
        < lax.broadcasted_iota(jnp.int32, (rows, rows), 1)
    ).astype(f32).astype(bf16)
    earlier = dot(chosen.astype(bf16), before, NN)
    rank = jnp.sum(earlier * chosen, axis=0, keepdims=True).astype(jnp.int32)
    sid = slot_ids(targets, rank, where_ref[0], where_ref[1], slots)
    sid_ref[...] = sid
    local = (image & (cap - 1)).astype(f32)
    line = lax.broadcasted_iota(jnp.int32, (16, rows), 0)
    views = views_ref[...]
    slot = lax.broadcasted_iota(jnp.int32, (slots, rows), 0)
    outs = [own_ref, core_ref] + [far_ref.at[where_ref[1] ^ m] for m in range(2, mates)]
    for m, out_ref in enumerate(outs):
        hots = [(slot == sid - (q * mates + m) * slots).astype(f32).astype(bf16) for q in range(parts)]
        packed = dot(jnp.concatenate(hots, axis=0), views, NN)
        lines = jnp.zeros((16, slots), f32)
        for q, hot in enumerate(hots):
            info = jnp.where(line == q, local, jnp.where(line == parts + q, 1.0, 0.0)).astype(bf16)
            lines += dot(info, hot, NT)
        out_ref[: parts * slots, :] = packed.astype(bf16)
        out_ref[parts * slots :, :] = jnp.zeros((16, width), bf16)
        out_ref[parts * slots :, :slots] = lines.astype(bf16)


def caption_kernel(counts, weight_ref, *refs):
    feats, (half_ref, unit_ref, inverse_ref, turned_ref) = refs[:-4], refs[-4:]

    def block(pieces):
        value = jnp.concatenate([ref[...] for ref in pieces], axis=0)
        embed = dot(value, weight_ref[...], NN)
        inverse = lax.rsqrt(jnp.sum(embed * embed, axis=1, keepdims=True) + epsilon)
        unit = embed * inverse
        half_ref[...] = unit.astype(bf16)
        unit_ref[...] = unit
        inverse_ref[...] = jnp.broadcast_to(inverse, inverse_ref.shape)
        turned_ref[...] = value.T

    start = 0
    for k, count in enumerate(counts):
        pl.when(pl.program_id(0) == k)(functools.partial(block, feats[start : start + count]))
        start += count


def score_kernel(cap, q, parts, priors, place_ref, scale_ref, offset_ref, a_ref, b_ref, ia_ref, ib_ref, count_ref, caps_ref, *refs):
    prior_refs, (va_ref, vb_ref, turned_ref, half_ref, loss_ref, pair_ref) = refs[:-6], refs[-6:]
    pair, slots = loss_ref.shape[:2]
    caps, width = caps_ref.shape
    scale, offset = scale_ref[0], offset_ref[0]
    eye = lax.broadcasted_iota(jnp.int32, (slots, slots), 0) == lax.broadcasted_iota(
        jnp.int32, (slots, slots), 1
    )
    held = [
        dot(eye.astype(f32).astype(bf16), ref[:, :slots], NT) for ref in (ia_ref, ib_ref)
    ]
    held = jnp.concatenate(held, axis=0)
    column = jnp.where(held[:, parts + q : parts + q + 1] > 0.5, held[:, q : q + 1], -1.0)
    named = lax.broadcasted_iota(jnp.int32, (pair * slots, cap), 1).astype(f32) == column
    weight = jnp.sum(
        jnp.where(named, 1.0 / count_ref[...].astype(f32), 0.0), axis=1, keepdims=True
    )
    factor = weight * scale
    x = jnp.concatenate([a_ref[...], b_ref[...]], axis=0).astype(f32)
    inverse = lax.rsqrt(jnp.sum(x * x, axis=1, keepdims=True) + epsilon)
    unit = x * inverse
    half = unit.astype(bf16)
    half_ref[: pair * slots, :] = half
    half_ref[pair * slots :, :] = jnp.zeros((half_ref.shape[0] - pair * slots, width), bf16)
    loss = jnp.zeros((pair * slots, 1), f32)
    for k in range(caps // cap):
        here = pl.ds(k * cap, cap)
        value = dot(half, caps_ref[here, :], NT) * scale + offset
        if k == 0:
            margin = jnp.where(named, -value, value)
        else:
            margin = value
        e = jnp.exp(-jnp.abs(margin))
        u = 1.0 + e
        r = 1.0 / u
        log1p = jnp.log(u) + (e - (u - 1.0)) * r
        loss = loss + jnp.sum(jnp.maximum(margin, 0.0) + log1p, axis=1, keepdims=True)
        grad = factor * jnp.where(margin >= 0.0, r, e * r)
        if k == 0:
            grad = jnp.where(named, -grad, grad)
        pair_ref[:, here] = grad.astype(bf16)
        turned_ref[here, : pair * slots] = grad.T.astype(bf16)
        turned_ref[here, pair * slots :] = jnp.zeros((cap, turned_ref.shape[1] - pair * slots), bf16)
    grad_x = dot(pair_ref[...], caps_ref[...], NN)
    grad_v = (grad_x - unit * jnp.sum(unit * grad_x, axis=1, keepdims=True)) * inverse
    grad_v = grad_v.astype(bf16)
    loss = loss * (1.0 / caps)
    for m, back_ref in enumerate((va_ref, vb_ref)):
        back_ref[:slots, :] = grad_v[m * slots : (m + 1) * slots]
    for m in range(pair):
        loss_ref[m] = jnp.broadcast_to(loss[m * slots : (m + 1) * slots], (slots, 128))
    if va_ref.shape[0] > slots:
        ones = jnp.ones((16, slots), bf16)
        line = lax.broadcasted_iota(jnp.int32, (16, slots), 0)
        for m, back_ref in enumerate((va_ref, vb_ref)):
            columns = [(p, ref[m][:, 0:1]) for p, ref in zip(priors, prior_refs)]
            columns.append((q, loss[m * slots : (m + 1) * slots]))
            lines = jnp.zeros((16, slots), f32)
            for p, value in columns:
                lines += jnp.where(line == p, dot(ones, jnp.where(eye, value, 0.0).astype(bf16), NN), 0.0)
            back_ref[slots:, :] = jnp.zeros((16, width), bf16)
            back_ref[slots:, :slots] = lines.astype(bf16)


def caption_grad_kernel(cap, pa_ref, pb_ref, xa_ref, xb_ref, unit_ref, inverse_ref, out_ref):
    half = jnp.concatenate([xa_ref[...], xb_ref[...]], axis=0)
    blocks = [pl.ds(start, cap) for start in range(0, out_ref.shape[0], cap)]
    totals = [dot(jnp.concatenate([pa_ref[here, :], pb_ref[here, :]], axis=1), half, NN) for here in blocks]
    for here, total in zip(blocks, totals):
        unit = unit_ref[here, :]
        total = total - unit * jnp.sum(unit * total, axis=1, keepdims=True)
        out_ref[here, :] = (total * inverse_ref[here, 0:1]).astype(bf16)


def unpack_kernel(slots, parts, part, sid_ref, *refs):
    backs, refs = refs[:mates], refs[mates:]
    rows = sid_ref.shape[1]
    last = len(refs) > 1
    many = mates * slots
    sid = jnp.broadcast_to(sid_ref[...].astype(f32), (128, rows)).T[:, 0:1].astype(jnp.int32)
    lanes = lax.broadcasted_iota(jnp.int32, (rows, many), 1)

    def hot(q):
        return (lanes == sid - q * many).astype(f32).astype(bf16)

    back = jnp.concatenate([ref[:slots, :] for ref in backs], axis=0)
    result = dot(hot(part), back, NN)
    if last:
        lines, (before_ref, out_ref, loss_ref) = refs[:mates], refs[mates:]
        result = result + before_ref[...].astype(f32)
    else:
        (out_ref,) = refs
    out_ref[...] = result.astype(bf16)
    if last:
        losses = jnp.zeros((16, rows), f32)
        for q in range(parts):
            line = jnp.concatenate([ref[:, :slots] for ref in lines], axis=1)
            mine = lax.broadcasted_iota(jnp.int32, line.shape, 0) == q
            line = jnp.where(mine, line.astype(f32), 0.0).astype(bf16)
            losses += dot(line, hot(q), NT)
        loss_ref[...] = jnp.sum(losses, axis=0, keepdims=True)


def after(value, *others):
    return lax.optimization_barrier((value, *others))[0]


def with_order(kernel, count, start=0):
    return lambda *refs: kernel(*refs[:start], *refs[start + count :])


ANY = pl.BlockSpec(memory_space=pl.ANY)


def cost(flops, read, wrote):
    return pl.CostEstimate(flops=flops, bytes_accessed=read + wrote, transcendentals=0)


def local(view_embeds, view_image, view_counts, text_feats, head_weight, logit_scale, logit_bias):
    cap = view_counts.shape[0]
    rows, width = view_embeds.shape
    groups = lax.axis_size("group")
    loops = lax.axis_size("loop")
    parts = groups // mates
    slots = -(-(11 * cap // (2 * groups)) // 16) * 16
    pair_slots = -(-2 * slots // 128) * 128
    caps = cap * loops
    me = lax.axis_index("group")
    lane = lax.axis_index("loop")
    cluster, place = me // mates, me % mates

    def over(axis, size, value, mask):
        return lax.ppermute(value, axis, [(i, i ^ mask) for i in range(size)])

    def over_loop(value, mask):
        return over("loop", loops, value, mask)

    def over_group(value, mask):
        return over("group", groups, value, mask)

    def bits_of(k):
        return [1 << b for b in range(k.bit_length()) if k >> b & 1][:2]

    in_order = sorted(range(1, loops), key=lambda k: (bin(k).count("1"), k))

    def gather_loop(block, *before):
        pieces = {0: [block]}
        for k in in_order:
            bits = bits_of(k)
            if len(bits) == 1:
                pieces[k] = [over_loop(block, k)]
                continue
            pieces[k] = []
            for i, bit in enumerate(bits):
                source = pieces[k ^ bit]
                half = source[i] if len(source) == 2 else lax.slice_in_dim(source[0], i * cap // 2, (i + 1) * cap // 2)
                pieces[k].append(over_loop(after(half, *before) if before else half, bit))
        return pieces

    def scatter_loop_at_once(terms):
        got = [over_loop(terms[k], k) for k in range(1, loops)]
        return got, lambda: (sum([value.astype(f32) for value in got], terms[0].astype(f32)), [])

    def scatter_loop(terms):
        half = cap // 2
        total = {(k, i): terms[k, i * half : (i + 1) * half] for k in range(loops) for i in range(2)}
        bit = {(k, i): bits_of(k)[i % len(bits_of(k))] for k, i in total if k}
        children = {at: [way for way in bit if way[1] == at[1] and way[0] ^ bit[way] == at[0]] for at in total}

        def depth(at):
            return 1 + max((depth(child) for child in children[at]), default=-1)

        waves = {}
        for at in bit:
            waves.setdefault((depth(at), bit[at]), []).append(at)
        first = min(level for level, _ in waves)

        def run(levels, *before):
            marks = []
            for (level, way), members in sorted(waves.items()):
                if (level == first) != levels:
                    continue
                sent = [total[at].astype(bf16) for at in members]
                sent = jnp.concatenate(sent) if len(sent) > 1 else sent[0]
                got = over_loop(after(sent, *before) if before else sent, way)
                marks.append(got)
                for n, (k, i) in enumerate(members):
                    parent = (k ^ way, i)
                    total[parent] = total[parent].astype(f32) + got[n * half : (n + 1) * half].astype(f32)
            return marks

        def finish(*before):
            marks = run(False, *before)
            return jnp.concatenate([total[0, 0], total[0, 1]], axis=0), marks

        return run(True), finish

    where = jnp.stack([cluster, place]).astype(jnp.int32)

    feats = [text_feats] + [over_group(text_feats, mates * q) for q in range(1, parts)]
    counts = [view_counts] + [over_group(view_counts, mates * q) for q in range(1, parts)]
    counts = [value.reshape(1, cap) for value in counts]

    def exchange(value):
        return lax.all_to_all(
            value, "group", split_axis=0, concat_axis=0, tiled=True,
            axis_index_groups=[list(range(i, i + mates)) for i in range(0, groups, mates)],
        )

    block = (parts * slots + 16, width)
    sid, own_rows, core_rows, far_rows = pl.pallas_call(
        functools.partial(pack_kernel, cap, groups, slots, parts),
        out_shape=[
            jax.ShapeDtypeStruct((1, rows), jnp.int32),
            jax.ShapeDtypeStruct(block, bf16),
            jax.ShapeDtypeStruct(block, bf16),
            jax.ShapeDtypeStruct((mates, *block), bf16),
        ],
        in_specs=[SMEM, VMEM, VMEM],
        out_specs=[VMEM] * 4,
        compiler_params=params(61),
        cost_estimate=cost(
            2 * mates * parts * slots * rows * width, rows * width * 2, mates * parts * slots * width * 2
        ),
        name="pack",
    )(where, view_image.reshape(1, rows), view_embeds)
    core_rows = over_group(core_rows, 1)
    gathered = [gather_loop(feats[0])]
    held = exchange(after(far_rows, *feats[1:], *[piece for k in range(1, loops) for piece in gathered[0][k]]))
    near_rows = [own_rows[None], core_rows[None]]
    origin = jnp.zeros((2,), jnp.int32)
    far_places = jnp.stack([place ^ 2, place ^ 3]).astype(jnp.int32)

    def caption(q, gathered, *before):
        pieces = [piece for k in range(loops) for piece in gathered[k]]
        return pl.pallas_call(
            with_order(functools.partial(caption_kernel, [len(gathered[k]) for k in range(loops)]), len(before)),
            grid=(loops,),
            out_shape=[
                jax.ShapeDtypeStruct((caps, width), bf16),
                jax.ShapeDtypeStruct((caps, width), f32),
                jax.ShapeDtypeStruct((caps, 128), f32),
                jax.ShapeDtypeStruct((width, caps), bf16),
            ],
            in_specs=[ANY] * len(before)
            + [pl.BlockSpec(value.shape, lambda k: (0, 0)) for value in [head_weight, *pieces]],
            out_specs=[pl.BlockSpec((cap, wide), lambda k: (k, 0)) for wide in (width, width, 128)]
            + [pl.BlockSpec((width, cap), lambda k: (0, k))],
            compiler_params=params(61),
            cost_estimate=cost(2 * caps * width * width, (caps + width) * width * 2, caps * width * 8),
            name="captions",
        )(*before, head_weight, *pieces)

    def score(q, sources, places, losses, *before):
        carry = len(losses) == parts - 1
        priors = list(losses) if carry else []
        sent = jax.ShapeDtypeStruct((slots + (16 if carry else 0), width), bf16)
        info = parts * slots // 16
        return pl.pallas_call(
            with_order(functools.partial(score_kernel, cap, q, parts, priors), len(before), 1),
            out_shape=[
                sent,
                sent,
                jax.ShapeDtypeStruct((caps, pair_slots), bf16),
                jax.ShapeDtypeStruct((pair_slots, width), bf16),
                jax.ShapeDtypeStruct((2, slots, 128), f32),
            ],
            grid_spec=pltpu.PrefetchScalarGridSpec(
                num_scalar_prefetch=1,
                grid=(1,),
                in_specs=[ANY] * len(before)
                + [
                    SMEM,
                    SMEM,
                    pl.BlockSpec((None, slots, width), lambda i, at: (at[0], q, 0)),
                    pl.BlockSpec((None, slots, width), lambda i, at: (at[1], q, 0)),
                    pl.BlockSpec((None, 16, width), lambda i, at: (at[0], info, 0)),
                    pl.BlockSpec((None, 16, width), lambda i, at: (at[1], info, 0)),
                    pl.BlockSpec((1, cap), lambda i, at: (0, 0)),
                    pl.BlockSpec((caps, width), lambda i, at: (0, 0)),
                ]
                + [pl.BlockSpec((2, slots, 128), lambda i, at: (0, 0, 0))] * len(priors),
                out_specs=[
                    pl.BlockSpec(sent.shape, lambda i, at: (0, 0)),
                    pl.BlockSpec(sent.shape, lambda i, at: (0, 0)),
                    pl.BlockSpec((caps, pair_slots), lambda i, at: (0, 0)),
                    pl.BlockSpec((pair_slots, width), lambda i, at: (0, 0)),
                    pl.BlockSpec((2, slots, 128), lambda i, at: (0, 0, 0)),
                ],
                scratch_shapes=[pltpu.VMEM((2 * slots, caps), bf16)],
            ),
            compiler_params=params(61),
            cost_estimate=cost(8 * slots * caps * width, (2 * slots + caps) * width * 2, slots * width * 12),
            name="score",
        )(
            places, *before, logit_scale, logit_bias, *sources, *sources, counts[q], captions[q][0],
            *[losses[p] for p in priors],
        )

    def caption_grad(q, near, far, *before):
        step = 2 * cap
        return pl.pallas_call(
            with_order(functools.partial(caption_grad_kernel, cap), len(before)),
            grid=(caps // step,),
            out_shape=jax.ShapeDtypeStruct((caps, width), bf16),
            in_specs=[ANY] * len(before)
            + [
                pl.BlockSpec((step, pair_slots), lambda k: (k, 0)),
                pl.BlockSpec((step, pair_slots), lambda k: (k, 0)),
                pl.BlockSpec((pair_slots, width), lambda k: (0, 0)),
                pl.BlockSpec((pair_slots, width), lambda k: (0, 0)),
                pl.BlockSpec((step, width), lambda k: (k, 0)),
                pl.BlockSpec((step, 128), lambda k: (k, 0)),
            ],
            out_specs=pl.BlockSpec((step, width), lambda k: (k, 0)),
            compiler_params=params(61),
            cost_estimate=cost(
                2 * mates * slots * caps * width, caps * width * 4 + mates * slots * width * 4, caps * width * 2
            ),
            name="caption_grad",
        )(*before, near[2], far[2], near[3], far[3], captions[q][1], captions[q][2])

    def unpack(q, result, *before):
        last = result is not None
        whole = pl.BlockSpec((rows, width), lambda i: (0, 0))
        line = pl.BlockSpec((1, rows), lambda i: (0, 0))
        return pl.pallas_call(
            with_order(functools.partial(unpack_kernel, slots, parts, q), len(before)),
            grid=(1,),
            out_shape=[jax.ShapeDtypeStruct((rows, width), bf16)]
            + [jax.ShapeDtypeStruct((1, rows), f32)] * last,
            in_specs=[ANY] * len(before)
            + [line]
            + [pl.BlockSpec((slots, width), lambda i: (0, 0))] * mates
            + [pl.BlockSpec((16, width), lambda i: (slots // 16, 0))] * (mates * last)
            + [whole] * last,
            out_specs=[whole] + [line] * last,
            compiler_params=params(61),
            cost_estimate=cost(2 * mates * slots * rows * width, mates * slots * width * 2, rows * width * 2),
            name="unpack",
        )(*before, sid, *back[q], *(carriers + [result] if last else []))

    captions, near, far, grads, back, finish, marks = {}, {}, {}, {}, {}, {}, {}
    there = {q: {} for q in range(parts)}
    token = [core_rows]
    for q in range(parts):
        if q:
            gathered.append({0: [feats[q]], **{k: [over_loop(feats[q], k)] for k in range(1, loops)}})
        captions[q] = caption(q, gathered[q], *token)
        near[q] = score(q, near_rows, origin, {p: near[p][4] for p in near})
        there[q][1] = over_group(near[q][1], 1)
        token = [near[q][4]] + ([there[q][1]] if q < parts - 1 else [])
    for q in reversed(range(parts)):
        far[q] = score(q, [held, held], far_places, {p: far[p][4] for p in far}, *token)
        there[q][2], there[q][3] = over_group(far[q][0], 2), over_group(far[q][1], 3)
        back[q] = [near[q][0], there[q][1], there[q][2], there[q][3]]
        grads[q] = caption_grad(q, near[q], far[q], *(back[q + 1][2:] if q + 1 in back else []))
        token = [grads[q], there[q][1]]
        marks[q], finish[q] = scatter_loop_at_once(grads[q].reshape(loops, cap, width))
    carriers = back[parts - 1][:2] + back[0][2:]

    sent = [finish[q]()[0].astype(bf16) for q in range(1, parts)]
    others = [over_group(value, mates * (q + 1)) for q, value in enumerate(sent)]

    share = width // groups
    head = sum(
        dot(captions[q][3], grads[q], NN) for q in range(parts)
    )
    head = head.astype(bf16)
    head = after(head, *sent, *back[parts - 1][2:])
    head = head.reshape(groups // 2, 2, share, width)
    core = me % 2
    got = over_group(lax.dynamic_index_in_dim(head, 1 - core, 1, keepdims=False), 1)
    head = lax.dynamic_index_in_dim(head, core, 1, keepdims=False).astype(f32) + got.astype(f32)
    head = head.astype(bf16).reshape(groups // 2, loops, share // loops, width)
    head = lax.all_to_all(jnp.swapaxes(head, 0, 1), "loop", split_axis=0, concat_axis=0, tiled=True)
    result = None
    for q in reversed(range(1, parts)):
        result = unpack(q, result[0] if result else None, got)
    head = jnp.sum(after(head, result[0], back[0][2]).astype(f32), axis=0).astype(bf16)
    head = lax.all_to_all(
        head, "group", split_axis=0, concat_axis=0, tiled=True,
        axis_index_groups=[list(range(i, groups, 2)) for i in range(2)],
    )
    piece = jnp.sum(head.astype(f32), axis=0).astype(bf16)

    total, waves = finish[0]()
    for other in others:
        total = total + other.astype(f32)
    text_grad = jnp.einsum(
        "cd,ed->ce", total.astype(bf16), head_weight, preferred_element_type=f32
    ).astype(bf16)

    copies = [over_loop(piece, k) for k in range(1, loops)]
    whole = jnp.stack([piece] + copies)
    whole = whole[lane ^ jnp.arange(loops, dtype=jnp.int32)]
    head_grad = whole.reshape(share, width).astype(f32)

    view_grad, view_loss = unpack(0, result[0], *copies)
    view_loss = view_loss.reshape(rows).astype(bf16)
    return (view_grad, view_loss, text_grad, head_grad)


def solution(mesh):
    return jax.shard_map(
        local,
        mesh=mesh,
        in_specs=(
            P(("loop", "group"), None),
            P(("loop", "group")),
            P(("loop", "group")),
            P(("loop", "group"), None),
            P(),
            P(),
            P(),
        ),
        out_specs=(
            P(("loop", "group"), None),
            P(("loop", "group")),
            P(("loop", "group"), None),
            P("group", None),
        ),
        check_vma=False,
    )
```

```python
import functools

import jax
import jax.numpy as jnp
from jax import lax
from jax.experimental import pallas as pl
from jax.experimental.pallas import tpu as pltpu
from jax.sharding import PartitionSpec as P

epsilon = 1e-06
mates = 4
f32 = jnp.float32
bf16 = jnp.bfloat16
NN = (((1,), (0,)), ((), ()))
NT = (((1,), (1,)), ((), ()))


def dot(a, b, dims):
    return lax.dot_general(a, b, dims, preferred_element_type=f32)


def params(mib, **more):
    return pltpu.CompilerParams(vmem_limit_bytes=mib << 20, **more)


VMEM = pl.BlockSpec(memory_space=pltpu.VMEM)
SMEM = pl.BlockSpec(memory_space=pltpu.SMEM)


def log2_of(value):
    bits = value.bit_length() - 1
    assert 1 << bits == value
    return bits


def slot_ids(targets, rank, cluster, place, slots):
    mate = (targets & (mates - 1)) ^ place
    q = (targets >> 2) ^ cluster
    return (q * mates + mate) * slots + rank


def pack_kernel(cap, groups, slots, parts, where_ref, image_ref, views_ref, sid_ref, own_ref, core_ref, far_ref):
    rows, width = views_ref.shape
    image = image_ref[...]
    targets = (image >> log2_of(cap)) & (groups - 1)
    wide = max(groups, 16)
    chosen = (lax.broadcasted_iota(jnp.int32, (wide, rows), 0) == targets).astype(f32)
    before = (
        lax.broadcasted_iota(jnp.int32, (rows, rows), 0)
        < lax.broadcasted_iota(jnp.int32, (rows, rows), 1)
    ).astype(f32).astype(bf16)
    earlier = dot(chosen.astype(bf16), before, NN)
    rank = jnp.sum(earlier * chosen, axis=0, keepdims=True).astype(jnp.int32)
    sid = slot_ids(targets, rank, where_ref[0], where_ref[1], slots)
    sid_ref[...] = sid
    local = (image & (cap - 1)).astype(f32)
    line = lax.broadcasted_iota(jnp.int32, (16, rows), 0)
    views = views_ref[...]
    slot = lax.broadcasted_iota(jnp.int32, (slots, rows), 0)
    outs = [own_ref, core_ref] + [far_ref.at[where_ref[1] ^ m] for m in range(2, mates)]
    for m, out_ref in enumerate(outs):
        hots = [(slot == sid - (q * mates + m) * slots).astype(f32).astype(bf16) for q in range(parts)]
        packed = dot(jnp.concatenate(hots, axis=0), views, NN)
        lines = jnp.zeros((16, slots), f32)
        for q, hot in enumerate(hots):
            info = jnp.where(line == q, local, jnp.where(line == parts + q, 1.0, 0.0)).astype(bf16)
            lines += dot(info, hot, NT)
        out_ref[: parts * slots, :] = packed.astype(bf16)
        out_ref[parts * slots :, :] = jnp.zeros((16, width), bf16)
        out_ref[parts * slots :, :slots] = lines.astype(bf16)


def caption_kernel(counts, weight_ref, *refs):
    feats, (half_ref, unit_ref, inverse_ref, turned_ref) = refs[:-4], refs[-4:]

    def block(pieces):
        value = jnp.concatenate([ref[...] for ref in pieces], axis=0)
        embed = dot(value, weight_ref[...], NN)
        inverse = lax.rsqrt(jnp.sum(embed * embed, axis=1, keepdims=True) + epsilon)
        unit = embed * inverse
        half_ref[...] = unit.astype(bf16)
        unit_ref[...] = unit
        inverse_ref[...] = jnp.broadcast_to(inverse, inverse_ref.shape)
        turned_ref[...] = value.T

    start = 0
    for k, count in enumerate(counts):
        pl.when(pl.program_id(0) == k)(functools.partial(block, feats[start : start + count]))
        start += count


def score_kernel(cap, q, parts, priors, place_ref, scale_ref, offset_ref, a_ref, b_ref, ia_ref, ib_ref, count_ref, caps_ref, *refs):
    prior_refs, (va_ref, vb_ref, turned_ref, half_ref, loss_ref, pair_ref) = refs[:-6], refs[-6:]
    pair, slots = loss_ref.shape[:2]
    caps, width = caps_ref.shape
    scale, offset = scale_ref[0], offset_ref[0]
    eye = lax.broadcasted_iota(jnp.int32, (slots, slots), 0) == lax.broadcasted_iota(
        jnp.int32, (slots, slots), 1
    )
    held = [
        dot(eye.astype(f32).astype(bf16), ref[:, :slots], NT) for ref in (ia_ref, ib_ref)
    ]
    held = jnp.concatenate(held, axis=0)
    column = jnp.where(held[:, parts + q : parts + q + 1] > 0.5, held[:, q : q + 1], -1.0)
    named = lax.broadcasted_iota(jnp.int32, (pair * slots, cap), 1).astype(f32) == column
    weight = jnp.sum(
        jnp.where(named, 1.0 / count_ref[...].astype(f32), 0.0), axis=1, keepdims=True
    )
    factor = weight * scale
    x = jnp.concatenate([a_ref[...], b_ref[...]], axis=0).astype(f32)
    inverse = lax.rsqrt(jnp.sum(x * x, axis=1, keepdims=True) + epsilon)
    unit = x * inverse
    half = unit.astype(bf16)
    half_ref[: pair * slots, :] = half
    half_ref[pair * slots :, :] = jnp.zeros((half_ref.shape[0] - pair * slots, width), bf16)
    loss = jnp.zeros((pair * slots, 1), f32)
    for k in range(caps // cap):
        here = pl.ds(k * cap, cap)
        value = dot(half, caps_ref[here, :], NT) * scale + offset
        if k == 0:
            margin = jnp.where(named, -value, value)
        else:
            margin = value
        e = jnp.exp(-jnp.abs(margin))
        u = 1.0 + e
        r = 1.0 / u
        log1p = jnp.log(u) + (e - (u - 1.0)) * r
        loss = loss + jnp.sum(jnp.maximum(margin, 0.0) + log1p, axis=1, keepdims=True)
        grad = factor * jnp.where(margin >= 0.0, r, e * r)
        if k == 0:
            grad = jnp.where(named, -grad, grad)
        pair_ref[:, here] = grad.astype(bf16)
        turned_ref[here, : pair * slots] = grad.T.astype(bf16)
        turned_ref[here, pair * slots :] = jnp.zeros((cap, turned_ref.shape[1] - pair * slots), bf16)
    grad_x = dot(pair_ref[...], caps_ref[...], NN)
    grad_v = (grad_x - unit * jnp.sum(unit * grad_x, axis=1, keepdims=True)) * inverse
    grad_v = grad_v.astype(bf16)
    loss = loss * (1.0 / caps)
    for m, back_ref in enumerate((va_ref, vb_ref)):
        back_ref[:slots, :] = grad_v[m * slots : (m + 1) * slots]
    for m in range(pair):
        loss_ref[m] = jnp.broadcast_to(loss[m * slots : (m + 1) * slots], (slots, 128))
    if va_ref.shape[0] > slots:
        ones = jnp.ones((16, slots), bf16)
        line = lax.broadcasted_iota(jnp.int32, (16, slots), 0)
        for m, back_ref in enumerate((va_ref, vb_ref)):
            columns = [(p, ref[m][:, 0:1]) for p, ref in zip(priors, prior_refs)]
            columns.append((q, loss[m * slots : (m + 1) * slots]))
            lines = jnp.zeros((16, slots), f32)
            for p, value in columns:
                lines += jnp.where(line == p, dot(ones, jnp.where(eye, value, 0.0).astype(bf16), NN), 0.0)
            back_ref[slots:, :] = jnp.zeros((16, width), bf16)
            back_ref[slots:, :slots] = lines.astype(bf16)


def caption_grad_kernel(cap, pa_ref, pb_ref, xa_ref, xb_ref, unit_ref, inverse_ref, out_ref):
    half = jnp.concatenate([xa_ref[...], xb_ref[...]], axis=0)
    blocks = [pl.ds(start, cap) for start in range(0, out_ref.shape[0], cap)]
    totals = [dot(jnp.concatenate([pa_ref[here, :], pb_ref[here, :]], axis=1), half, NN) for here in blocks]
    for here, total in zip(blocks, totals):
        unit = unit_ref[here, :]
        total = total - unit * jnp.sum(unit * total, axis=1, keepdims=True)
        out_ref[here, :] = (total * inverse_ref[here, 0:1]).astype(bf16)


def unpack_kernel(slots, parts, part, sid_ref, *refs):
    backs, refs = refs[:mates], refs[mates:]
    rows = sid_ref.shape[1]
    last = len(refs) > 1
    many = mates * slots
    sid = jnp.broadcast_to(sid_ref[...].astype(f32), (128, rows)).T[:, 0:1].astype(jnp.int32)
    lanes = lax.broadcasted_iota(jnp.int32, (rows, many), 1)

    def hot(q):
        return (lanes == sid - q * many).astype(f32).astype(bf16)

    back = jnp.concatenate([ref[:slots, :] for ref in backs], axis=0)
    result = dot(hot(part), back, NN)
    if last:
        lines, (before_ref, out_ref, loss_ref) = refs[:mates], refs[mates:]
        result = result + before_ref[...].astype(f32)
    else:
        (out_ref,) = refs
    out_ref[...] = result.astype(bf16)
    if last:
        losses = jnp.zeros((16, rows), f32)
        for q in range(parts):
            line = jnp.concatenate([ref[:, :slots] for ref in lines], axis=1)
            mine = lax.broadcasted_iota(jnp.int32, line.shape, 0) == q
            line = jnp.where(mine, line.astype(f32), 0.0).astype(bf16)
            losses += dot(line, hot(q), NT)
        losses = jnp.sum(losses, axis=0, keepdims=True)
        for i in range(rows // 128):
            loss_ref[i : i + 1, :] = losses[:, i * 128 : (i + 1) * 128]


def after(value, *others):
    return lax.optimization_barrier((value, *others))[0]


def with_order(kernel, count, start=0):
    return lambda *refs: kernel(*refs[:start], *refs[start + count :])


ANY = pl.BlockSpec(memory_space=pl.ANY)


def cost(flops, read, wrote):
    return pl.CostEstimate(flops=flops, bytes_accessed=read + wrote, transcendentals=0)


def local(view_embeds, view_image, view_counts, text_feats, head_weight, logit_scale, logit_bias):
    cap = view_counts.shape[0]
    rows, width = view_embeds.shape
    groups = lax.axis_size("group")
    loops = lax.axis_size("loop")
    parts = groups // mates
    slots = -(-(11 * cap // (2 * groups)) // 16) * 16
    pair_slots = -(-2 * slots // 128) * 128
    caps = cap * loops
    me = lax.axis_index("group")
    lane = lax.axis_index("loop")
    cluster, place = me // mates, me % mates

    def over(axis, size, value, mask):
        return lax.ppermute(value, axis, [(i, i ^ mask) for i in range(size)])

    def over_loop(value, mask):
        return over("loop", loops, value, mask)

    def over_group(value, mask):
        return over("group", groups, value, mask)

    def bits_of(k):
        return [1 << b for b in range(k.bit_length()) if k >> b & 1][:2]

    in_order = sorted(range(1, loops), key=lambda k: (bin(k).count("1"), k))

    def gather_loop(block, *before):
        pieces = {0: [block]}
        for k in in_order:
            bits = bits_of(k)
            if len(bits) == 1:
                pieces[k] = [over_loop(block, k)]
                continue
            pieces[k] = []
            for i, bit in enumerate(bits):
                source = pieces[k ^ bit]
                half = source[i] if len(source) == 2 else lax.slice_in_dim(source[0], i * cap // 2, (i + 1) * cap // 2)
                pieces[k].append(over_loop(after(half, *before) if before else half, bit))
        return pieces

    def scatter_loop_at_once(terms):
        got = [over_loop(terms[k], k) for k in range(1, loops)]
        return got, lambda: (sum([value.astype(f32) for value in got], terms[0].astype(f32)), [])

    def scatter_loop(terms):
        half = cap // 2
        total = {(k, i): terms[k, i * half : (i + 1) * half] for k in range(loops) for i in range(2)}
        bit = {(k, i): bits_of(k)[i % len(bits_of(k))] for k, i in total if k}
        children = {at: [way for way in bit if way[1] == at[1] and way[0] ^ bit[way] == at[0]] for at in total}

        def depth(at):
            return 1 + max((depth(child) for child in children[at]), default=-1)

        waves = {}
        for at in bit:
            waves.setdefault((depth(at), bit[at]), []).append(at)
        first = min(level for level, _ in waves)

        def run(levels, *before):
            marks = []
            for (level, way), members in sorted(waves.items()):
                if (level == first) != levels:
                    continue
                sent = [total[at].astype(bf16) for at in members]
                sent = jnp.concatenate(sent) if len(sent) > 1 else sent[0]
                got = over_loop(after(sent, *before) if before else sent, way)
                marks.append(got)
                for n, (k, i) in enumerate(members):
                    parent = (k ^ way, i)
                    total[parent] = total[parent].astype(f32) + got[n * half : (n + 1) * half].astype(f32)
            return marks

        def finish(*before):
            marks = run(False, *before)
            return jnp.concatenate([total[0, 0], total[0, 1]], axis=0), marks

        return run(True), finish

    where = jnp.stack([cluster, place]).astype(jnp.int32)

    feats = [text_feats] + [over_group(text_feats, mates * q) for q in range(1, parts)]
    counts = [view_counts] + [over_group(view_counts, mates * q) for q in range(1, parts)]
    counts = [value.reshape(1, cap) for value in counts]

    def exchange(value):
        return lax.all_to_all(
            value, "group", split_axis=0, concat_axis=0, tiled=True,
            axis_index_groups=[list(range(i, i + mates)) for i in range(0, groups, mates)],
        )

    block = (parts * slots + 16, width)
    sid, own_rows, core_rows, far_rows = pl.pallas_call(
        functools.partial(pack_kernel, cap, groups, slots, parts),
        out_shape=[
            jax.ShapeDtypeStruct((1, rows), jnp.int32),
            jax.ShapeDtypeStruct(block, bf16),
            jax.ShapeDtypeStruct(block, bf16),
            jax.ShapeDtypeStruct((mates, *block), bf16),
        ],
        in_specs=[SMEM, VMEM, VMEM],
        out_specs=[VMEM] * 4,
        compiler_params=params(61),
        cost_estimate=cost(
            2 * mates * parts * slots * rows * width, rows * width * 2, mates * parts * slots * width * 2
        ),
        name="pack",
    )(where, view_image.reshape(1, rows), view_embeds)
    core_rows = over_group(core_rows, 1)
    gathered = [gather_loop(feats[0])]
    held = exchange(after(far_rows, *feats[1:], *[piece for k in range(1, loops) for piece in gathered[0][k]]))
    near_rows = [own_rows[None], core_rows[None]]
    origin = jnp.zeros((2,), jnp.int32)
    far_places = jnp.stack([place ^ 2, place ^ 3]).astype(jnp.int32)

    def caption(q, gathered, *before):
        pieces = [piece for k in range(loops) for piece in gathered[k]]
        return pl.pallas_call(
            with_order(functools.partial(caption_kernel, [len(gathered[k]) for k in range(loops)]), len(before)),
            grid=(loops,),
            out_shape=[
                jax.ShapeDtypeStruct((caps, width), bf16),
                jax.ShapeDtypeStruct((caps, width), f32),
                jax.ShapeDtypeStruct((caps, 128), f32),
                jax.ShapeDtypeStruct((width, caps), bf16),
            ],
            in_specs=[ANY] * len(before)
            + [pl.BlockSpec(value.shape, lambda k: (0, 0)) for value in [head_weight, *pieces]],
            out_specs=[pl.BlockSpec((cap, wide), lambda k: (k, 0)) for wide in (width, width, 128)]
            + [pl.BlockSpec((width, cap), lambda k: (0, k))],
            compiler_params=params(61),
            cost_estimate=cost(2 * caps * width * width, (caps + width) * width * 2, caps * width * 8),
            name="captions",
        )(*before, head_weight, *pieces)

    def score(q, sources, places, losses, *before):
        carry = len(losses) == parts - 1
        priors = list(losses) if carry else []
        sent = jax.ShapeDtypeStruct((slots + (16 if carry else 0), width), bf16)
        info = parts * slots // 16
        return pl.pallas_call(
            with_order(functools.partial(score_kernel, cap, q, parts, priors), len(before), 1),
            out_shape=[
                sent,
                sent,
                jax.ShapeDtypeStruct((caps, pair_slots), bf16),
                jax.ShapeDtypeStruct((pair_slots, width), bf16),
                jax.ShapeDtypeStruct((2, slots, 128), f32),
            ],
            grid_spec=pltpu.PrefetchScalarGridSpec(
                num_scalar_prefetch=1,
                grid=(1,),
                in_specs=[ANY] * len(before)
                + [
                    SMEM,
                    SMEM,
                    pl.BlockSpec((None, slots, width), lambda i, at: (at[0], q, 0)),
                    pl.BlockSpec((None, slots, width), lambda i, at: (at[1], q, 0)),
                    pl.BlockSpec((None, 16, width), lambda i, at: (at[0], info, 0)),
                    pl.BlockSpec((None, 16, width), lambda i, at: (at[1], info, 0)),
                    pl.BlockSpec((1, cap), lambda i, at: (0, 0)),
                    pl.BlockSpec((caps, width), lambda i, at: (0, 0)),
                ]
                + [pl.BlockSpec((2, slots, 128), lambda i, at: (0, 0, 0))] * len(priors),
                out_specs=[
                    pl.BlockSpec(sent.shape, lambda i, at: (0, 0)),
                    pl.BlockSpec(sent.shape, lambda i, at: (0, 0)),
                    pl.BlockSpec((caps, pair_slots), lambda i, at: (0, 0)),
                    pl.BlockSpec((pair_slots, width), lambda i, at: (0, 0)),
                    pl.BlockSpec((2, slots, 128), lambda i, at: (0, 0, 0)),
                ],
                scratch_shapes=[pltpu.VMEM((2 * slots, caps), bf16)],
            ),
            compiler_params=params(61),
            cost_estimate=cost(8 * slots * caps * width, (2 * slots + caps) * width * 2, slots * width * 12),
            name="score",
        )(
            places, *before, logit_scale, logit_bias, *sources, *sources, counts[q], captions[q][0],
            *[losses[p] for p in priors],
        )

    def caption_grad(q, near, far, *before):
        step = 2 * cap
        return pl.pallas_call(
            with_order(functools.partial(caption_grad_kernel, cap), len(before)),
            grid=(caps // step,),
            out_shape=jax.ShapeDtypeStruct((caps, width), bf16),
            in_specs=[ANY] * len(before)
            + [
                pl.BlockSpec((step, pair_slots), lambda k: (k, 0)),
                pl.BlockSpec((step, pair_slots), lambda k: (k, 0)),
                pl.BlockSpec((pair_slots, width), lambda k: (0, 0)),
                pl.BlockSpec((pair_slots, width), lambda k: (0, 0)),
                pl.BlockSpec((step, width), lambda k: (k, 0)),
                pl.BlockSpec((step, 128), lambda k: (k, 0)),
            ],
            out_specs=pl.BlockSpec((step, width), lambda k: (k, 0)),
            compiler_params=params(61),
            cost_estimate=cost(
                2 * mates * slots * caps * width, caps * width * 4 + mates * slots * width * 4, caps * width * 2
            ),
            name="caption_grad",
        )(*before, near[2], far[2], near[3], far[3], captions[q][1], captions[q][2])

    def unpack(q, result, *before):
        last = result is not None
        whole = pl.BlockSpec((rows, width), lambda i: (0, 0))
        line = pl.BlockSpec((1, rows), lambda i: (0, 0))
        return pl.pallas_call(
            with_order(functools.partial(unpack_kernel, slots, parts, q), len(before)),
            grid=(1,),
            out_shape=[jax.ShapeDtypeStruct((rows, width), bf16)]
            + [jax.ShapeDtypeStruct((rows // 128, 128), f32)] * last,
            in_specs=[ANY] * len(before)
            + [line]
            + [pl.BlockSpec((slots, width), lambda i: (0, 0))] * mates
            + [pl.BlockSpec((16, width), lambda i: (slots // 16, 0))] * (mates * last)
            + [whole] * last,
            out_specs=[whole] + [pl.BlockSpec((rows // 128, 128), lambda i: (0, 0))] * last,
            compiler_params=params(61),
            cost_estimate=cost(2 * mates * slots * rows * width, mates * slots * width * 2, rows * width * 2),
            name="unpack",
        )(*before, sid, *back[q], *(carriers + [result] if last else []))

    captions, near, far, grads, back, finish, marks = {}, {}, {}, {}, {}, {}, {}
    there = {q: {} for q in range(parts)}
    token = [core_rows]
    for q in range(parts):
        if q:
            gathered.append({0: [feats[q]], **{k: [over_loop(feats[q], k)] for k in range(1, loops)}})
        captions[q] = caption(q, gathered[q], *token)
        near[q] = score(q, near_rows, origin, {p: near[p][4] for p in near})
        there[q][1] = over_group(near[q][1], 1)
        token = [near[q][4]] + ([there[q][1]] if q < parts - 1 else [])
    for q in reversed(range(parts)):
        far[q] = score(q, [held, held], far_places, {p: far[p][4] for p in far}, *token)
        there[q][2], there[q][3] = over_group(far[q][0], 2), over_group(far[q][1], 3)
        back[q] = [near[q][0], there[q][1], there[q][2], there[q][3]]
        grads[q] = caption_grad(q, near[q], far[q], *(back[q + 1][2:] if q + 1 in back else []))
        token = [grads[q], there[q][1]]
        marks[q], finish[q] = scatter_loop_at_once(grads[q].reshape(loops, cap, width))
    carriers = back[parts - 1][:2] + back[0][2:]

    sent = [finish[q]()[0].astype(bf16) for q in range(1, parts)]
    others = [over_group(value, mates * (q + 1)) for q, value in enumerate(sent)]

    share = width // groups
    head = sum(
        dot(captions[q][3], grads[q], NN) for q in range(parts)
    )
    head = head.astype(bf16)
    head = after(head, *sent, *back[parts - 1][2:])
    head = head.reshape(groups // 2, 2, share, width)
    core = me % 2
    got = over_group(lax.dynamic_index_in_dim(head, 1 - core, 1, keepdims=False), 1)
    head = lax.dynamic_index_in_dim(head, core, 1, keepdims=False).astype(f32) + got.astype(f32)
    head = head.astype(bf16).reshape(groups // 2, loops, share // loops, width)
    head = lax.all_to_all(jnp.swapaxes(head, 0, 1), "loop", split_axis=0, concat_axis=0, tiled=True)
    result = None
    for q in reversed(range(1, parts)):
        result = unpack(q, result[0] if result else None, got)
    head = jnp.sum(after(head, result[0], back[0][2]).astype(f32), axis=0).astype(bf16)
    head = lax.all_to_all(
        head, "group", split_axis=0, concat_axis=0, tiled=True,
        axis_index_groups=[list(range(i, groups, 2)) for i in range(2)],
    )
    piece = jnp.sum(head.astype(f32), axis=0).astype(bf16)

    total, waves = finish[0]()
    for other in others:
        total = total + other.astype(f32)
    text_grad = jnp.einsum(
        "cd,ed->ce", total.astype(bf16), head_weight, preferred_element_type=f32
    ).astype(bf16)

    copies = [over_loop(piece, k) for k in range(1, loops)]
    whole = jnp.stack([piece] + copies)
    whole = whole[lane ^ jnp.arange(loops, dtype=jnp.int32)]
    head_grad = whole.reshape(share, width).astype(f32)

    view_grad, view_loss = unpack(0, result[0], *copies)
    view_loss = view_loss.reshape(rows).astype(bf16)
    return (view_grad, view_loss, text_grad, head_grad)


def solution(mesh):
    return jax.shard_map(
        local,
        mesh=mesh,
        in_specs=(
            P(("loop", "group"), None),
            P(("loop", "group")),
            P(("loop", "group")),
            P(("loop", "group"), None),
            P(),
            P(),
            P(),
        ),
        out_specs=(
            P(("loop", "group"), None),
            P(("loop", "group")),
            P(("loop", "group"), None),
            P("group", None),
        ),
        check_vma=False,
    )
```
